256 devices in a mesh: gx: 4 (over y), gy: 4 (over x), gz: 16 (over z, core).
Axes of the slice: x: 4, y: 4, z: 8, core: 2. Of those that a mesh axis runs over, the one named last changes fastest.
Arguments:
- activations: bfloat16 [4, 4, 4, 16, 16, 64, 128], P('gx', 'gy', None, None, None, 'gz'), may hold values from -6 to 6
- cotangent: bfloat16 [4, 4, 4, 16, 16, 64, 128], P('gx', 'gy', None, None, None, 'gz'), may hold values from -6 to 6
- tap_weights: bfloat16 [9, 128, 128], replicated, may hold values from -0.1875 to 0.1875
- depth_tap_weight: bfloat16 [5, 128], replicated, may hold values from -2.5 to 2.5
- counts: int32 [4, 4], P('gx', 'gy'), may hold values from 2 to 4, as said below
- neighbors: int32 [4, 4, 4, 8], P('gx', 'gy'), may hold values from 0 to 36, as said below
Outputs:
- output: bfloat16 [4, 4, 4, 16, 16, 64, 128], P('gx', 'gy', None, None, None, 'gz')
- input_grad: bfloat16 [4, 4, 4, 16, 16, 64, 128], P('gx', 'gy', None, None, None, 'gz')
- tap_grad: float32 [9, 128, 128], replicated
- depth_grad: float32 [5, 128], replicated
The draws below stay inside these ranges and needn't reach their ends.
Inputs may be any that keep to these rules, and one draw needn't show every extreme that they name: Slots 0 to counts - 1 of an owner are occupied; one owner has all 4 slots occupied. `neighbors`: each owner holds a grid of 3 x 3 block column positions; the owners tile the plane along gx and gy. Directions d = 0..7 are (-1,-1), (-1,0), (-1,1), (0,-1), (0,1), (1,-1), (1,0), (1,1) in (x, y). For an occupied slot the entry names the occupied column at the adjacent position as ((ox' + 1) * 3 + oy' + 1) * 4 + slot, with (ox', oy') the offset of its owner; 36 marks an empty or outside position and every direction of an unoccupied slot. The relation is geometric, hence symmetric.
All inputs are finite; a program needn't handle non-finite values.
Results may differ from the reference program's by a relative error of at most 0.005.
Values may be sent and summed in bfloat16 or wider, within the bound.
A program may use at most 128 MiB of HBM per device.

```python
import jax
import jax.numpy as jnp
from jax import lax

C = 128
TILE = 16
SIDE = 3
CAP = 4
NZ = 64
DEPTH_DILATION = 16
N_GX = 4
N_GY = 4


DIRECTIONS = ((-1, -1), (-1, 0), (-1, 1), (0, -1), (0, 1), (1, -1), (1, 0), (1, 1))


def layout(key):
    owner_count = N_GX * N_GY
    key_perm, key_count, key_pick = jax.random.split(key, 3)
    perms = jax.vmap(lambda sub: jax.random.permutation(sub, SIDE * SIDE))(jax.random.split(key_perm, owner_count)).astype(jnp.int32)
    slot_counts = jax.random.randint(key_count, (owner_count,), CAP // 2, CAP + 1).astype(jnp.int32)
    picked = jax.random.randint(key_pick, (), 0, owner_count)
    slot_counts = jnp.where(jnp.arange(owner_count) == picked, CAP, slot_counts).astype(jnp.int32)
    ranks = jnp.argsort(perms, axis=1, stable=True).astype(jnp.int32)
    owner_ids = jnp.arange(owner_count, dtype=jnp.int32)
    owner_x = (owner_ids // N_GY)[:, None]
    owner_y = (owner_ids % N_GY)[:, None]
    slot_ids = jnp.arange(CAP, dtype=jnp.int32)[None, :]
    places = perms[:, :CAP]
    pos_x = owner_x * SIDE + places // SIDE
    pos_y = owner_y * SIDE + places % SIDE
    columns = []
    for step_x, step_y in DIRECTIONS:
        near_x = pos_x + step_x
        near_y = pos_y + step_y
        inside = (near_x >= 0) & (near_x < N_GX * SIDE) & (near_y >= 0) & (near_y < N_GY * SIDE)
        clip_x = jnp.clip(near_x, 0, N_GX * SIDE - 1)
        clip_y = jnp.clip(near_y, 0, N_GY * SIDE - 1)
        other_x = clip_x // SIDE
        other_y = clip_y // SIDE
        other_owner = other_x * N_GY + other_y
        other_place = (clip_x - other_x * SIDE) * SIDE + (clip_y - other_y * SIDE)
        rank_there = ranks[other_owner, other_place]
        alive = inside & (rank_there < slot_counts[other_owner]) & (slot_ids < slot_counts[:, None])
        code = (other_x - owner_x + 1) * 3 + (other_y - owner_y) + 1
        columns.append(jnp.where(alive, code * CAP + rank_there, 9 * CAP))
    table = jnp.stack(columns, axis=-1).astype(jnp.int32).reshape(N_GX, N_GY, CAP, 8)
    return (slot_counts.reshape(N_GX, N_GY), table)


def draw_counts(key, part):
    slot_counts, table = layout(key)
    return slot_counts


def draw_neighbors(key, part):
    slot_counts, table = layout(key)
    return table


def steps_of(stream_key, extent, pieces, low, high):
    loudness = 1.0
    for axis_at, shards_of in pieces:
        steps = jax.random.uniform(jax.random.fold_in(jax.random.fold_in(stream_key, 6), axis_at), (shards_of,), jnp.float32, low / len(pieces), high / len(pieces))
        loudness = loudness * jnp.repeat(jnp.exp(steps), extent[axis_at] // shards_of).reshape((-1,) + (1,) * (len(extent) - 1 - axis_at))
    return loudness


def normal_values(own_key, dims, scale, limit, pieces=(), kind=jnp.bfloat16):
    result = scale * jax.random.normal(own_key, dims, jnp.float32)
    if pieces:
        result = result * steps_of(own_key, dims, pieces, -0.22, 0.18)
    return jnp.clip(result, -limit, limit).astype(kind)


def setup_inputs(seed: int = 0) -> dict:
    keys = jax.random.split(jax.random.key(seed), 7)
    return {
        "activations": normal_values(keys[0], (N_GX, N_GY, CAP, TILE, TILE, NZ, C), 1.0, 6.0, ((0, 4), (1, 4), (5, 16))),
        "cotangent": normal_values(keys[1], (N_GX, N_GY, CAP, TILE, TILE, NZ, C), 1.0, 6.0, ((0, 4), (1, 4), (5, 16))),
        "tap_weights": normal_values(keys[2], (9, C, C), (9 * C) ** -0.5, 0.1875),
        "depth_tap_weight": normal_values(keys[3], (5, C), 0.5, 2.5),
        "counts": draw_counts(jax.random.fold_in(keys[6], 71), 0),
        "neighbors": draw_neighbors(jax.random.fold_in(keys[6], 71), 0),
    }


def rims_of(tile):
    last_idx = tile.shape[-4] - 1
    edge_rows = jnp.concatenate([tile[..., 0, :, :, :], tile[..., last_idx, :, :, :], tile[..., :, 0, :, :], tile[..., :, last_idx, :, :]], axis=-3)
    corner_cells = jnp.stack([tile[..., 0, 0, :, :], tile[..., 0, last_idx, :, :], tile[..., last_idx, 0, :, :], tile[..., last_idx, last_idx, :, :]], axis=-3)
    return jnp.concatenate([edge_rows, corner_cells], axis=-3)


def assemble(center, pooled, neighbor_ids):
    tile_len = center.shape[1]
    chosen = [pooled[neighbor_ids[:, direction]] for direction in range(8)]

    def edge_of(direction, which):
        return chosen[direction][:, which * tile_len:(which + 1) * tile_len]

    def corner_of(direction, which):
        return chosen[direction][:, 4 * tile_len + which:4 * tile_len + which + 1]

    top_row = jnp.concatenate([corner_of(0, 3), edge_of(1, 1), corner_of(2, 2)], axis=1)
    bottom_row = jnp.concatenate([corner_of(5, 1), edge_of(6, 0), corner_of(7, 0)], axis=1)
    middle = jnp.concatenate([edge_of(3, 3)[:, :, None], center, edge_of(4, 2)[:, :, None]], axis=2)
    return jnp.concatenate([top_row[:, None], middle, bottom_row[:, None]], axis=1)


def convolve(padded, tap_weights):
    tile_len = padded.shape[1] - 2
    channels = padded.shape[-1]
    shape_out = padded.shape[:1] + (tile_len, tile_len) + padded.shape[3:]
    summed = jnp.zeros(shape_out, jnp.float32)
    for row_tap in range(3):
        for col_tap in range(3):
            window = padded[:, row_tap:row_tap + tile_len, col_tap:col_tap + tile_len]
            summed = summed + jnp.dot(window.reshape(-1, channels), tap_weights[3 * row_tap + col_tap], preferred_element_type=jnp.float32).reshape(shape_out)
    return summed


def convolve_back(padded, tap_weights):
    tile_len = padded.shape[1] - 2
    channels = padded.shape[-1]
    shape_out = padded.shape[:1] + (tile_len, tile_len) + padded.shape[3:]
    summed = jnp.zeros(shape_out, jnp.float32)
    for row_tap in range(3):
        for col_tap in range(3):
            window = padded[:, 2 - row_tap:2 - row_tap + tile_len, 2 - col_tap:2 - col_tap + tile_len]
            summed = summed + jnp.dot(window.reshape(-1, channels), tap_weights[3 * row_tap + col_tap].T, preferred_element_type=jnp.float32).reshape(shape_out)
    return summed


def tap_gradient(padded, grad_center):
    tile_len = padded.shape[1] - 2
    channels = padded.shape[-1]
    grad_rows = grad_center.reshape(-1, channels)
    parts = []
    for row_tap in range(3):
        for col_tap in range(3):
            window = padded[:, row_tap:row_tap + tile_len, col_tap:col_tap + tile_len]
            parts.append(lax.dot_general(window.reshape(-1, channels), grad_rows, (((0,), (0,)), ((), ())), preferred_element_type=jnp.float32))
    return jnp.stack(parts, axis=0)


def z_padded(field, dilation):
    widths = [(0, 0)] * field.ndim
    widths[-2] = (2 * dilation, 2 * dilation)
    return jnp.pad(field, widths)


def depth_forward_pass(field, depth_tap_weight, dilation):
    length = field.shape[-2]
    padded = z_padded(field, dilation)
    summed = jnp.zeros(field.shape, jnp.float32)
    for tap_idx in range(5):
        window = lax.slice_in_dim(padded, tap_idx * dilation, tap_idx * dilation + length, axis=field.ndim - 2)
        summed = summed + depth_tap_weight[tap_idx].astype(jnp.float32) * window.astype(jnp.float32)
    return summed


def depth_backward_pass(field, depth_tap_weight, dilation):
    length = field.shape[-2]
    padded = z_padded(field, dilation)
    summed = jnp.zeros(field.shape, jnp.float32)
    for tap_idx in range(5):
        start = (4 - tap_idx) * dilation
        window = lax.slice_in_dim(padded, start, start + length, axis=field.ndim - 2)
        summed = summed + depth_tap_weight[tap_idx].astype(jnp.float32) * window.astype(jnp.float32)
    return summed


def depth_weight_gradient(active_columns, grads, dilation):
    length = active_columns.shape[-2]
    padded = z_padded(active_columns, dilation)
    grads_float = grads.astype(jnp.float32)
    axes_all = tuple(range(active_columns.ndim - 1))
    parts = []
    for tap_idx in range(5):
        window = lax.slice_in_dim(padded, tap_idx * dilation, tap_idx * dilation + length, axis=active_columns.ndim - 2)
        parts.append(jnp.sum(window.astype(jnp.float32) * grads_float, axis=axes_all))
    return jnp.stack(parts, axis=0)


def reference(activations, cotangent, tap_weights, depth_tap_weight, counts, neighbors):
    slot_ids = jnp.arange(CAP, dtype=jnp.int32)
    live_all = slot_ids[None, None, :] < counts[:, :, None]
    masked = jnp.where(live_all[:, :, :, None, None, None, None], activations, jnp.zeros((), activations.dtype))
    rim_x = jnp.pad(rims_of(masked), ((1, 1), (1, 1), (0, 0), (0, 0), (0, 0), (0, 0)))
    owners = jnp.arange(N_GX * N_GY, dtype=jnp.int32)

    def neighborhood(rim_pad, owner_x, owner_y):
        zero = jnp.zeros((), jnp.int32)
        near = lax.dynamic_slice(rim_pad, (owner_x, owner_y, zero, zero, zero, zero), (3, 3) + rim_pad.shape[2:])
        pooled = near.reshape((9 * CAP,) + near.shape[3:])
        return jnp.concatenate([pooled, jnp.zeros((1,) + pooled.shape[1:], pooled.dtype)], axis=0)

    def forward_owner(owner_id):
        owner_x = owner_id // N_GY
        owner_y = owner_id % N_GY
        center = masked[owner_x, owner_y]
        live_float = (slot_ids < counts[owner_x, owner_y]).astype(jnp.float32)[:, None, None, None, None]
        padded_x = assemble(center, neighborhood(rim_x, owner_x, owner_y), neighbors[owner_x, owner_y])
        pre_act = convolve(padded_x, tap_weights)
        active_columns = (jax.nn.silu(pre_act) * live_float).astype(jnp.bfloat16)
        depth_output = depth_forward_pass(active_columns, depth_tap_weight, DEPTH_DILATION).astype(jnp.bfloat16)
        output = (center.astype(jnp.float32) + depth_output.astype(jnp.float32)).astype(jnp.bfloat16)
        gradient_column = cotangent[owner_x, owner_y]
        depth_reverse_pass = depth_backward_pass(gradient_column, depth_tap_weight, DEPTH_DILATION).astype(jnp.bfloat16)
        depth_partial = depth_weight_gradient(active_columns, gradient_column, DEPTH_DILATION)
        sigma = jax.nn.sigmoid(pre_act)
        grad_pre = (depth_reverse_pass.astype(jnp.float32) * sigma * (1.0 + pre_act * (1.0 - sigma)) * live_float).astype(jnp.bfloat16)
        return output, grad_pre, depth_partial

    outputs, grad_pres, depth_parts = lax.map(forward_owner, owners)
    shape_all = (N_GX, N_GY) + outputs.shape[1:]
    grad_all = grad_pres.reshape(shape_all)
    rim_g = jnp.pad(rims_of(grad_all), ((1, 1), (1, 1), (0, 0), (0, 0), (0, 0), (0, 0)))

    def backward_owner(owner_id):
        owner_x = owner_id // N_GY
        owner_y = owner_id % N_GY
        live_float = (slot_ids < counts[owner_x, owner_y]).astype(jnp.float32)[:, None, None, None, None]
        table = neighbors[owner_x, owner_y]
        padded_x = assemble(masked[owner_x, owner_y], neighborhood(rim_x, owner_x, owner_y), table)
        grad_center = grad_all[owner_x, owner_y]
        padded_g = assemble(grad_center, neighborhood(rim_g, owner_x, owner_y), table)
        back_conv = convolve_back(padded_g, tap_weights)
        input_grad = ((cotangent[owner_x, owner_y].astype(jnp.float32) + back_conv) * live_float).astype(jnp.bfloat16)
        return input_grad, tap_gradient(padded_x, grad_center)

    input_grads, tap_parts = lax.map(backward_owner, owners)
    return (outputs.reshape(shape_all), input_grads.reshape(shape_all), jnp.sum(tap_parts, axis=0), jnp.sum(depth_parts, axis=0))
```

```python
import functools

import jax
import jax.numpy as jnp
from jax import lax
from jax.experimental import pallas as pl
from jax.experimental.pallas import tpu as pltpu
from jax.sharding import PartitionSpec as P

MESH = pl.DeviceIdType.MESH
F32 = jnp.float32
BF16 = jnp.bfloat16

SLOTS = 4
EDGE = 16
ZS = 4
LINE = EDGE * ZS
ROWS = EDGE * LINE
C = 128
GROUP = 4
PART = ROWS // GROUP
PLANE = 16
NZ = 16
CHIPS = 8
HALF = 5
TAPS = 9


def kernel(
    counts_hbm,
    nbr_hbm,
    act_hbm,
    cot_hbm,
    w_hbm,
    dw_hbm,
    out_hbm,
    ig_hbm,
    tg_hbm,
    dg_hbm,
    counts_ref,
    nbr_ref,
    act_v,
    cot_v,
    w_v,
    dw_ref,
    wbt,
    pad,
    xcat,
    gcat,
    gt,
    dsilu,
    active,
    cot_cols,
    back_send,
    back,
    act_cols,
    fwd_send,
    fwd,
    x_top,
    x_bot,
    x_left,
    x_right,
    g_top,
    g_bot,
    g_left,
    g_right,
    corner_send,
    corner_recv,
    col0,
    col1,
    corner_f,
    tacc,
    tp,
    rs_buf,
    z_src,
    c_buf,
    z_buf,
    z_all,
    dg_acc,
    dg_pair,
    dg_plane,
    dg_z,
    dg_out,
    load_sem,
    store_sem,
    halo_send,
    halo_recv,
    a2a_send,
    a2a_recv,
    pl_send,
    pl_recv,
    core_send,
    core_recv,
    chip_send,
    chip_recv,
):
    gx = lax.axis_index("gx")
    gy = lax.axis_index("gy")
    gz = lax.axis_index("gz")
    me_p = gx * 4 + gy
    q = gz // 4

    loads = [
        pltpu.make_async_copy(act_hbm, act_v, load_sem.at[0]),
        pltpu.make_async_copy(cot_hbm, cot_v, load_sem.at[1]),
        pltpu.make_async_copy(w_hbm, w_v, load_sem.at[2]),
        pltpu.make_async_copy(
            cot_hbm.at[:, pl.ds(pl.multiple_of(q * PART, PART), PART)], cot_cols.at[q], load_sem.at[3]
        ),
        pltpu.make_async_copy(dw_hbm, dw_ref, load_sem.at[4]),
        pltpu.make_async_copy(counts_hbm, counts_ref, load_sem.at[5]),
        pltpu.make_async_copy(nbr_hbm, nbr_ref, load_sem.at[6]),
    ]
    for load in loads:
        load.start()

    chip = gz // 2
    core = gz % 2

    def chip_peer(j):
        return {"gz": (gz + 2 * j) % NZ}

    core_peer = {"gz": gz + 1 - 2 * core}

    def p_peer(j):
        p = (me_p + j) % PLANE
        return {"gx": p // 4, "gy": p % 4}

    barrier = pltpu.get_barrier_semaphore()

    pl.semaphore_signal(barrier, inc=1, device_id=core_peer, device_id_type=MESH)
    for j in range(1, CHIPS):
        pl.semaphore_signal(barrier, inc=1, device_id=chip_peer(j), device_id_type=MESH)
    for j in range(1, PLANE):
        pl.semaphore_signal(barrier, inc=1, device_id=p_peer(j), device_id_type=MESH)
    pl.semaphore_wait(barrier, CHIPS + PLANE - 1)

    def group_peer(o):
        return {"gz": (gz + 4 * o) % NZ}

    def part_of(k):
        return pl.ds(pl.multiple_of(k * PART, PART), PART)

    def gather_copy(which, src, dst, s, o):
        k = (q + o) % GROUP
        return pltpu.make_async_remote_copy(
            src_ref=src.at[s, part_of(k)],
            dst_ref=dst.at[q, s],
            send_sem=a2a_send.at[which, s, o],
            recv_sem=a2a_recv.at[which, s, o],
            device_id=group_peer(o),
            device_id_type=MESH,
        )

    def spread_copy(which, src, dst, s, o):
        k = (q + o) % GROUP
        return pltpu.make_async_remote_copy(
            src_ref=src.at[k, s],
            dst_ref=dst.at[s, part_of(q)],
            send_sem=a2a_send.at[which, s, o],
            recv_sem=a2a_recv.at[which, s, o],
            device_id=group_peer(o),
            device_id_type=MESH,
        )

    cot_gather = functools.partial(gather_copy, 0, cot_hbm, cot_cols)
    back_spread = functools.partial(spread_copy, 1, back_send, back)
    act_gather = functools.partial(gather_copy, 2, active, act_cols)
    fwd_spread = functools.partial(spread_copy, 3, fwd_send, fwd)

    def start_all(copy, s):
        for o in range(1, GROUP):
            copy(s, o).start()

    def recv_all(copy, s):
        for o in range(1, GROUP):
            copy(s, o).wait_recv()

    for s in range(SLOTS):
        start_all(cot_gather, s)

    pools = ((x_top, x_bot, x_left, x_right), (g_top, g_bot, g_left, g_right))

    def halo_copies(f):
        def shift(axis, at, step):
            return {axis: (at + step + 4) % 4}

        def copy(k, src, dst, dev):
            return pltpu.make_async_remote_copy(
                src_ref=src,
                dst_ref=dst,
                send_sem=halo_send.at[f, k],
                recv_sem=halo_recv.at[f, k],
                device_id=dev,
                device_id_type=MESH,
            )

        result = []
        p_top, p_bot, p_left, p_right = pools[f]
        for k, (pool, axis, at, step) in enumerate(
            ((p_top, "gx", gx, 1), (p_bot, "gx", gx, -1), (p_left, "gy", gy, 1), (p_right, "gy", gy, -1))
        ):
            result.append(
                copy(k, pool.at[pl.ds(0, SLOTS)], pool.at[pl.ds(SLOTS, SLOTS)], shift(axis, at, step))
            )
        for k, (dx, dy) in enumerate(((1, 1), (1, -1), (-1, 1), (-1, -1))):
            dev = {**shift("gx", gx, dx), **shift("gy", gy, dy)}
            result.append(copy(4 + k, corner_send.at[f, k], corner_recv.at[f, k], dev))
        return result

    def own_pools(f):
        p_top, p_bot, p_left, p_right = pools[f]
        for s in range(SLOTS):
            p_bot[s] = pad[s, 1, 8 : 8 + LINE].astype(BF16)
            p_top[s] = pad[s, EDGE, 8 : 8 + LINE].astype(BF16)
            for x in range(EDGE):
                col0[ZS * x : ZS * x + ZS] = pad[s, 1 + x, 8:12]
                col1[ZS * x : ZS * x + ZS] = pad[s, 1 + x, 68:72]
            p_right[s] = col0[...].astype(BF16)
            p_left[s] = col1[...].astype(BF16)
            for k, (x, at) in enumerate(((EDGE, 68), (EDGE, 8), (1, 68), (1, 8))):
                corner_f[k, ZS * s : ZS * s + ZS] = pad[s, x, at : at + ZS]
        for k in range(4):
            corner_send[f, k] = corner_f[k].astype(BF16)
        for pool in (p_top, p_bot, p_left, p_right):
            pool[2 * SLOTS] = jnp.zeros((LINE, C), BF16)

    def entry(code, other):
        own = (code >= 16) & (code < 20)
        far = (code >= other) & (code < other + 4)
        return jnp.where(own, code - 16, jnp.where(far, code - other + 4, 8))

    def fill_halo(f, s):
        p_top, p_bot, p_left, p_right = pools[f]
        codes = [nbr_ref[s, d] for d in range(8)]
        pad[s, 0, 8 : 8 + LINE] = p_top[entry(codes[1], 4)].astype(F32)
        pad[s, EDGE + 1, 8 : 8 + LINE] = p_bot[entry(codes[6], 28)].astype(F32)
        col0[...] = p_left[entry(codes[3], 12)].astype(F32)
        col1[...] = p_right[entry(codes[4], 20)].astype(F32)
        for x in range(EDGE):
            pad[s, 1 + x, 4:8] = col0[ZS * x : ZS * x + ZS]
            pad[s, 1 + x, 72:76] = col1[ZS * x : ZS * x + ZS]
        for k, (d, row, at, pool_x, base_x, end_x, pool_y, base_y, end_y, base_c) in enumerate(
            (
                (0, 0, 4, p_top, 4, 1, p_left, 12, 1, 0),
                (2, 0, 72, p_top, 4, 0, p_right, 20, 1, 8),
                (5, EDGE + 1, 4, p_bot, 28, 1, p_left, 12, 0, 24),
                (7, EDGE + 1, 72, p_bot, 28, 0, p_right, 20, 0, 32),
            )
        ):
            code = codes[d]

            def piece(pool, base, end):
                low = (LINE - 16) * end
                rows = pool[entry(code, base), low : low + 16].astype(F32)
                return rows[12:16] if end else rows[0:4]

            via_x = piece(pool_x, base_x, end_x)
            via_y = piece(pool_y, base_y, end_y)
            tile = corner_recv[f, k].astype(F32)
            value = via_x
            value = jnp.where((code >= base_y) & (code < base_y + 4), via_y, value)
            for m in range(SLOTS):
                value = jnp.where(code == base_c + m, tile[ZS * m : ZS * m + ZS], value)
            pad[s, row, at : at + ZS] = value

    def lay_out(s, dst):
        for x in range(EDGE + 2):
            for j in range(3):
                at = 4 + ZS * j
                dst[s, x, :, C * j : C * j + C] = pad[s, x, at : at + LINE].astype(BF16)

    loads[0].wait()
    loads[5].wait()
    loads[6].wait()
    count = counts_ref[0, 0]

    def centre_x(s, carry):
        live = s < count
        for x in range(EDGE):
            rows = act_v[s, LINE * x : LINE * x + LINE].astype(F32)
            pad[s, 1 + x, 8 : 8 + LINE] = jnp.where(live, rows, 0.0)
        return carry

    lax.fori_loop(0, SLOTS, centre_x, 0)
    own_pools(0)
    x_halo = halo_copies(0)
    for copy in x_halo:
        copy.start()
    loads[2].wait()
    for i in range(3):
        for j in range(3):
            wbt[i, :, C * j : C * j + C] = w_v[3 * (2 - i) + 2 - j]

    for copy in x_halo:
        copy.wait_recv()

    def build_x(s, carry):
        fill_halo(0, s)
        lay_out(s, xcat)
        return carry

    lax.fori_loop(0, SLOTS, build_x, 0)

    def conv(n, carry):
        s = n // GROUP
        b = n % GROUP
        total = jnp.zeros((PART, C), F32)
        for i in range(3):
            window = xcat[s, pl.ds(4 * b + i, 4)].reshape(PART, 3 * C)
            weights = w_v[3 * i : 3 * i + 3].reshape(3 * C, C)
            total = total + jnp.dot(window, weights, preferred_element_type=F32)
        live = (s < count).astype(F32)
        sigma = jax.nn.sigmoid(total)
        active[s, part_of(b)] = (total * sigma * live).astype(BF16)
        dsilu[s, part_of(b)] = sigma * (1.0 + total * (1.0 - sigma)) * live
        return carry

    lax.fori_loop(0, SLOTS * GROUP, conv, 0)
    own_cols = pltpu.make_async_copy(active.at[:, part_of(q)], act_cols.at[q], load_sem.at[0])
    own_cols.start()

    loads[4].wait()
    taps = [dw_ref[t : t + 1].astype(F32) for t in range(5)]
    STEP = 32

    loads[3].wait()

    def depth_back(s):
        def step(n, carry):
            rows = pl.ds(pl.multiple_of(n * STEP, STEP), STEP)
            col = [cot_cols[k, s, rows].astype(F32) for k in range(GROUP)]
            for k in range(GROUP):
                total = None
                for t in range(5):
                    src = k - (t - 2)
                    if 0 <= src < GROUP:
                        term = taps[t] * col[src]
                        total = term if total is None else total + term
                back_send[k, s, rows] = total.astype(BF16)
            return carry

        lax.fori_loop(0, PART // STEP, step, 0)

    def do_back(s, carry):
        recv_all(cot_gather, s)
        depth_back(s)
        start_all(back_spread, s)
        back[s, part_of(q)] = back_send[q, s]
        return carry

    lax.fori_loop(0, SLOTS, do_back, 0)
    for s in range(SLOTS):
        start_all(act_gather, s)

    tacc[...] = jnp.zeros_like(tacc)

    def do_grad(s, carry):
        recv_all(back_spread, s)
        for x in range(EDGE):
            rows = pl.ds(LINE * x, LINE)
            grad = (back[s, rows].astype(F32) * dsilu[s, rows]).astype(BF16)
            gt[s, rows] = grad
            pad[s, 1 + x, 8 : 8 + LINE] = grad.astype(F32)
        return carry

    def tap_step(s, carry):
        grad_t = gt[s].T
        for i in range(3):
            window = xcat[s, i : i + EDGE].reshape(ROWS, 3 * C)
            tacc[i] += jnp.dot(grad_t, window, preferred_element_type=F32)
        return carry

    def grad_slot(s, carry):
        do_grad(s, 0)
        tap_step(s, 0)
        return carry

    lax.fori_loop(0, SLOTS - 1, grad_slot, 0)
    do_grad(SLOTS - 1, 0)
    own_pools(1)
    g_halo = halo_copies(1)
    for copy in g_halo:
        copy.start()
    tap_step(SLOTS - 1, 0)
    for i in range(3):
        for j in range(3):
            block = tacc[i, :, C * j : C * j + C].T
            tp[:, 3 * i + j] = block.reshape(PLANE, 8, C)

    def plane_scatter(j):
        p = (me_p + j) % PLANE
        return pltpu.make_async_remote_copy(
            src_ref=tp.at[p],
            dst_ref=rs_buf.at[me_p],
            send_sem=pl_send.at[0, j],
            recv_sem=pl_recv.at[0, j],
            device_id=p_peer(j),
            device_id_type=MESH,
        )

    def plane_gather(j):
        return pltpu.make_async_remote_copy(
            src_ref=z_all.at[pl.ds(0, TAPS)],
            dst_ref=tg_hbm.at[:, me_p],
            send_sem=pl_send.at[1, j],
            recv_sem=pl_recv.at[1, j],
            device_id=p_peer(j),
            device_id_type=MESH,
        )

    def plane_depth(j):
        return pltpu.make_async_remote_copy(
            src_ref=dg_plane.at[me_p],
            dst_ref=dg_plane.at[me_p],
            send_sem=pl_send.at[2, j],
            recv_sem=pl_recv.at[2, j],
            device_id=p_peer(j),
            device_id_type=MESH,
        )

    def core_copy(n, src, dst):
        return pltpu.make_async_remote_copy(
            src_ref=src,
            dst_ref=dst,
            send_sem=core_send.at[n],
            recv_sem=core_recv.at[n],
            device_id=core_peer,
            device_id_type=MESH,
        )

    core_scatter = core_copy(0, z_src.at[pl.ds(HALF * (1 - core), HALF)], c_buf)
    core_gather = core_copy(1, z_all.at[pl.ds(HALF * core, HALF)], z_all.at[pl.ds(HALF * core, HALF)])
    core_depth = core_copy(2, dg_pair.at[core], dg_pair.at[core])

    def chip_copy(n, src, dst, j):
        return pltpu.make_async_remote_copy(
            src_ref=src,
            dst_ref=dst,
            send_sem=chip_send.at[n, j],
            recv_sem=chip_recv.at[n, j],
            device_id=chip_peer(j),
            device_id_type=MESH,
        )

    def chip_gather(j):
        return chip_copy(0, z_buf.at[chip], z_buf.at[chip], j)

    def chip_depth(j):
        return chip_copy(1, dg_z.at[chip], dg_z.at[chip], j)

    def each(copy, action, stop=PLANE):
        def step(j, carry):
            getattr(copy(j), action)()
            return carry

        lax.fori_loop(1, stop, step, 0)

    each(plane_scatter, "start")

    own_cols.wait()
    dg_acc[...] = jnp.zeros_like(dg_acc)

    def depth_forward(s):
        def step(n, carry):
            rows = pl.ds(pl.multiple_of(n * STEP, STEP), STEP)
            col = [act_cols[k, s, rows].astype(F32) for k in range(GROUP)]
            cot = [cot_cols[k, s, rows].astype(F32) for k in range(GROUP)]
            sums = [None] * 5
            for k in range(GROUP):
                total = None
                for t in range(5):
                    src = k + t - 2
                    if 0 <= src < GROUP:
                        term = taps[t] * col[src]
                        total = term if total is None else total + term
                        grad = col[src] * cot[k]
                        sums[t] = grad if sums[t] is None else sums[t] + grad
                fwd_send[k, s, rows] = total.astype(BF16)
            for t in range(5):
                dg_acc[t] += jnp.sum(sums[t].reshape(STEP // 8, 8, C), axis=0)
            return carry

        lax.fori_loop(0, PART // STEP, step, 0)

    def do_forward(s):
        recv_all(act_gather, s)
        depth_forward(s)
        start_all(fwd_spread, s)
        fwd[s, part_of(q)] = fwd_send[q, s]

    do_forward(0)

    for copy in g_halo:
        copy.wait_recv()

    def build_g(s, carry):
        fill_halo(1, s)
        lay_out(s, gcat)
        return carry

    lax.fori_loop(0, SLOTS, build_g, 0)

    loads[1].wait()

    def conv_back(n, carry):
        s = n // GROUP
        b = n % GROUP
        total = jnp.zeros((PART, C), F32)
        for i in range(3):
            window = gcat[s, pl.ds(4 * b + i, 4)].reshape(PART, 3 * C)
            total = total + lax.dot_general(
                window, wbt[i], (((1,), (1,)), ((), ())), preferred_element_type=F32
            )
        live = (s < count).astype(F32)
        rows = part_of(b)
        cot_v[s, rows] = ((cot_v[s, rows].astype(F32) + total) * live).astype(BF16)
        return carry

    lax.fori_loop(0, 2 * GROUP, conv_back, 0)

    rs_buf[me_p] = tp[me_p]
    z_src[...] = jnp.zeros_like(z_src)
    each(plane_scatter, "wait_recv")
    part_sum = rs_buf[0]
    for p in range(1, PLANE):
        part_sum = part_sum + rs_buf[p]
    z_src[0:TAPS] = part_sum
    core_scatter.start()
    core_scatter.wait_recv()
    z_buf[chip] = z_src[pl.ds(HALF * core, HALF)] + c_buf[...]
    each(chip_gather, "start", CHIPS)

    do_forward(1)
    lax.fori_loop(2 * GROUP, SLOTS * GROUP, conv_back, 0)
    ig_store = pltpu.make_async_copy(cot_v, ig_hbm, store_sem.at[0])
    ig_store.start()
    do_forward(2)
    do_forward(3)
    dg_pair[core] = jnp.concatenate(
        [jnp.sum(dg_acc[t], axis=0, keepdims=True) for t in range(5)] + [jnp.zeros((3, C), F32)], axis=0
    )
    core_depth.start()
    core_depth.wait_recv()
    dg_plane[me_p] = dg_pair[0] + dg_pair[1]
    each(plane_depth, "start")
    each(plane_depth, "wait_recv")
    dg_sum = dg_plane[0]
    for p in range(1, PLANE):
        dg_sum = dg_sum + dg_plane[p]
    dg_z[chip] = dg_sum
    each(chip_depth, "start", CHIPS)

    each(chip_gather, "wait_recv", CHIPS)
    z_sum = z_buf[0]
    for k in range(1, CHIPS):
        z_sum = z_sum + z_buf[k]
    z_all[pl.ds(HALF * core, HALF)] = z_sum
    core_gather.start()
    core_gather.wait_recv()
    each(plane_gather, "start")
    tg_own = pltpu.make_async_copy(z_all.at[pl.ds(0, TAPS)], tg_hbm.at[:, me_p], store_sem.at[1])
    tg_own.start()

    def out_store(s):
        return pltpu.make_async_copy(act_v.at[s], out_hbm.at[s], store_sem.at[2 + s])

    def finish(s, carry):
        recv_all(fwd_spread, s)
        live = s < count
        for b in range(GROUP):
            rows = pl.ds(PART * b, PART)
            masked = jnp.where(live, act_v[s, rows].astype(F32), 0.0)
            act_v[s, rows] = (masked + fwd[s, rows].astype(F32)).astype(BF16)
        out_store(s).start()
        return carry

    lax.fori_loop(0, SLOTS - 1, finish, 0)
    each(chip_depth, "wait_recv", CHIPS)
    dg_all = dg_z[0]
    for k in range(1, CHIPS):
        dg_all = dg_all + dg_z[k]
    dg_out[...] = dg_all[0:5]
    dg_store = pltpu.make_async_copy(dg_out, dg_hbm, store_sem.at[6])
    dg_store.start()
    finish(SLOTS - 1, 0)
    each(plane_gather, "wait_recv")

    for copy in x_halo + g_halo:
        copy.wait_send()
    for copy in (cot_gather, back_spread, act_gather, fwd_spread):
        for s in range(SLOTS):
            for o in range(1, GROUP):
                copy(s, o).wait_send()
    for copy in (plane_scatter, plane_gather, plane_depth):
        each(copy, "wait_send")
    for copy in (chip_gather, chip_depth):
        each(copy, "wait_send", CHIPS)
    for copy in (core_scatter, core_gather, core_depth):
        copy.wait_send()
    ig_store.wait()
    tg_own.wait()
    dg_store.wait()
    for s in range(SLOTS):
        out_store(s).wait()


def copy_out(*refs):
    src, dst, buf, load_sem, store_sem = refs[0:4], refs[4:8], refs[8:12], refs[12], refs[13]
    steps = [(0, s) for s in range(SLOTS)] + [(1, s) for s in range(SLOTS)] + [(2, s) for s in range(3)] + [(3, 0)]

    def at(k, ref, s):
        return ref.at[s] if k < 2 else ref.at[pl.ds(3 * s, 3)] if k == 2 else ref

    loads, stores = [], []
    for n, (k, s) in enumerate(steps):
        loads.append(pltpu.make_async_copy(at(k, src[k], s), at(k, buf[k], s), load_sem.at[n]))
        stores.append(pltpu.make_async_copy(at(k, buf[k], s), at(k, dst[k], s), store_sem.at[n]))
    for load in loads:
        load.start()
    for load, store in zip(loads, stores):
        load.wait()
        store.start()
    for store in stores:
        store.wait()


def body(activations, cotangent, tap_weights, depth_tap_weight, counts, neighbors):
    field = (SLOTS, ROWS, C)
    anywhere = pl.BlockSpec(memory_space=pl.ANY)
    results = pl.pallas_call(
        kernel,
        out_shape=[
            jax.ShapeDtypeStruct(field, BF16),
            jax.ShapeDtypeStruct(field, BF16),
            jax.ShapeDtypeStruct((TAPS, PLANE, 8, C), F32),
            jax.ShapeDtypeStruct((5, C), F32),
        ],
        in_specs=[anywhere] * 6,
        out_specs=[anywhere] * 4,
        scratch_shapes=[
            pltpu.SMEM((1, 1), jnp.int32),
            pltpu.SMEM((SLOTS, 8), jnp.int32),
            pltpu.VMEM(field, BF16),
            pltpu.VMEM(field, BF16),
            pltpu.VMEM((TAPS, C, C), BF16),
            pltpu.VMEM((5, C), BF16),
            pltpu.VMEM((3, C, 3 * C), BF16),
            pltpu.VMEM((SLOTS, EDGE + 2, LINE + 16, C), F32),
            pltpu.VMEM((SLOTS, EDGE + 2, LINE, 3 * C), BF16),
            pltpu.VMEM((SLOTS, EDGE + 2, LINE, 3 * C), BF16),
            pltpu.VMEM(field, BF16),
            pltpu.VMEM(field, F32),
            pltpu.VMEM(field, BF16),
            pltpu.VMEM((GROUP, SLOTS, PART, C), BF16),
            pltpu.VMEM((GROUP, SLOTS, PART, C), BF16),
            pltpu.VMEM(field, BF16),
            pltpu.VMEM((GROUP, SLOTS, PART, C), BF16),
            pltpu.VMEM((GROUP, SLOTS, PART, C), BF16),
            pltpu.VMEM(field, BF16),
            pltpu.VMEM((2 * SLOTS + 1, LINE, C), BF16),
            pltpu.VMEM((2 * SLOTS + 1, LINE, C), BF16),
            pltpu.VMEM((2 * SLOTS + 1, LINE, C), BF16),
            pltpu.VMEM((2 * SLOTS + 1, LINE, C), BF16),
            pltpu.VMEM((2 * SLOTS + 1, LINE, C), BF16),
            pltpu.VMEM((2 * SLOTS + 1, LINE, C), BF16),
            pltpu.VMEM((2 * SLOTS + 1, LINE, C), BF16),
            pltpu.VMEM((2 * SLOTS + 1, LINE, C), BF16),
            pltpu.VMEM((2, 4, 16, C), BF16),
            pltpu.VMEM((2, 4, 16, C), BF16),
            pltpu.VMEM((LINE, C), F32),
            pltpu.VMEM((LINE, C), F32),
            pltpu.VMEM((4, 16, C), F32),
            pltpu.VMEM((3, C, 3 * C), F32),
            pltpu.VMEM((PLANE, TAPS, 8, C), F32),
            pltpu.VMEM((PLANE, TAPS, 8, C), F32),
            pltpu.VMEM((2 * HALF, 8, C), F32),
            pltpu.VMEM((HALF, 8, C), F32),
            pltpu.VMEM((CHIPS, HALF, 8, C), F32),
            pltpu.VMEM((2 * HALF, 8, C), F32),
            pltpu.VMEM((5, 8, C), F32),
            pltpu.VMEM((2, 8, C), F32),
            pltpu.VMEM((PLANE, 8, C), F32),
            pltpu.VMEM((CHIPS, 8, C), F32),
            pltpu.VMEM((5, C), F32),
            pltpu.SemaphoreType.DMA((7,)),
            pltpu.SemaphoreType.DMA((7,)),
            pltpu.SemaphoreType.DMA((2, 8)),
            pltpu.SemaphoreType.DMA((2, 8)),
            pltpu.SemaphoreType.DMA((4, SLOTS, GROUP)),
            pltpu.SemaphoreType.DMA((4, SLOTS, GROUP)),
            pltpu.SemaphoreType.DMA((3, PLANE)),
            pltpu.SemaphoreType.DMA((3, PLANE)),
            pltpu.SemaphoreType.DMA((3,)),
            pltpu.SemaphoreType.DMA((3,)),
            pltpu.SemaphoreType.DMA((2, CHIPS)),
            pltpu.SemaphoreType.DMA((2, CHIPS)),
        ],
        compiler_params=pltpu.CompilerParams(
            collective_id=0, has_side_effects=True, vmem_limit_bytes=60 * 2**20
        ),
        name="unet_section",
    )(
        counts,
        neighbors.reshape(SLOTS, 8),
        activations.reshape(field),
        cotangent.reshape(field),
        tap_weights,
        depth_tap_weight,
    )
    output, input_grad, tap_grad, depth_grad = pl.pallas_call(
        copy_out,
        out_shape=[jax.ShapeDtypeStruct(r.shape, r.dtype) for r in results],
        in_specs=[anywhere] * 4,
        out_specs=[anywhere] * 4,
        scratch_shapes=[pltpu.VMEM(r.shape, r.dtype) for r in results]
        + [pltpu.SemaphoreType.DMA((12,)), pltpu.SemaphoreType.DMA((12,))],
        compiler_params=pltpu.CompilerParams(vmem_limit_bytes=60 * 2**20),
        name="copy_out",
    )(*results)
    return (
        output.reshape(activations.shape),
        input_grad.reshape(activations.shape),
        tap_grad.reshape(TAPS, C, C),
        depth_grad,
    )


def solution(mesh):
    field = P("gx", "gy", None, None, None, "gz", None)
    return jax.shard_map(
        body,
        mesh=mesh,
        in_specs=(field, field, P(), P(), P("gx", "gy"), P("gx", "gy", None, None)),
        out_specs=(field, field, P(), P()),
        check_vma=False,
    )
```

```python
import functools

import jax
import jax.numpy as jnp
from jax import lax
from jax.experimental import pallas as pl
from jax.experimental.pallas import tpu as pltpu
from jax.sharding import PartitionSpec as P

MESH = pl.DeviceIdType.MESH
F32 = jnp.float32
BF16 = jnp.bfloat16

SLOTS = 4
EDGE = 16
ZS = 4
LINE = EDGE * ZS
ROWS = EDGE * LINE
C = 128
GROUP = 4
PART = ROWS // GROUP
PLANE = 16
NZ = 16
CHIPS = 8
HALF = 5
TAPS = 9
PIECE = 80
ZPIECE = 48


def kernel(
    counts_hbm,
    nbr_hbm,
    act_hbm,
    cot_hbm,
    w_hbm,
    dw_hbm,
    out_hbm,
    ig_hbm,
    tg_hbm,
    dg_hbm,
    counts_ref,
    nbr_ref,
    act_v,
    cot_v,
    w_v,
    dw_ref,
    wbt,
    pad,
    xcat,
    gcat,
    gt,
    dsilu,
    active,
    cot_cols,
    back_send,
    back,
    act_cols,
    fwd_send,
    fwd,
    x_top,
    x_bot,
    x_left,
    x_right,
    g_top,
    g_bot,
    g_left,
    g_right,
    corner_send,
    corner_recv,
    col0,
    col1,
    corner_f,
    tacc,
    tp,
    tp_send,
    rs_buf,
    z_src,
    c_buf,
    z_buf,
    z_all,
    tg_send,
    dg_acc,
    dg_pair,
    dg_plane,
    dg_z,
    dg_out,
    load_sem,
    store_sem,
    halo_send,
    halo_recv,
    a2a_send,
    a2a_recv,
    pl_send,
    pl_recv,
    core_send,
    core_recv,
    chip_send,
    chip_recv,
):
    gx = lax.axis_index("gx")
    gy = lax.axis_index("gy")
    gz = lax.axis_index("gz")
    me_p = gx * 4 + gy
    q = gz // 4

    loads = [
        pltpu.make_async_copy(act_hbm, act_v, load_sem.at[0]),
        pltpu.make_async_copy(cot_hbm, cot_v, load_sem.at[1]),
        pltpu.make_async_copy(w_hbm, w_v, load_sem.at[2]),
        pltpu.make_async_copy(
            cot_hbm.at[:, pl.ds(pl.multiple_of(q * PART, PART), PART)], cot_cols.at[q], load_sem.at[3]
        ),
        pltpu.make_async_copy(dw_hbm, dw_ref, load_sem.at[4]),
        pltpu.make_async_copy(counts_hbm, counts_ref, load_sem.at[5]),
        pltpu.make_async_copy(nbr_hbm, nbr_ref, load_sem.at[6]),
    ]
    for load in loads:
        load.start()

    chip = gz // 2
    core = gz % 2

    def chip_peer(j):
        return {"gz": (gz + 2 * j) % NZ}

    core_peer = {"gz": gz + 1 - 2 * core}

    def p_peer(j):
        p = (me_p + j) % PLANE
        return {"gx": p // 4, "gy": p % 4}

    barrier = pltpu.get_barrier_semaphore()

    pl.semaphore_signal(barrier, inc=1, device_id=core_peer, device_id_type=MESH)
    for j in range(1, CHIPS):
        pl.semaphore_signal(barrier, inc=1, device_id=chip_peer(j), device_id_type=MESH)
    for j in range(1, PLANE):
        pl.semaphore_signal(barrier, inc=1, device_id=p_peer(j), device_id_type=MESH)
    pl.semaphore_wait(barrier, CHIPS + PLANE - 1)

    def group_peer(o):
        return {"gz": (gz + 4 * o) % NZ}

    def part_of(k):
        return pl.ds(pl.multiple_of(k * PART, PART), PART)

    def gather_copy(which, src, dst, s, o):
        k = (q + o) % GROUP
        return pltpu.make_async_remote_copy(
            src_ref=src.at[s, part_of(k)],
            dst_ref=dst.at[q, s],
            send_sem=a2a_send.at[which, s, o],
            recv_sem=a2a_recv.at[which, s, o],
            device_id=group_peer(o),
            device_id_type=MESH,
        )

    def spread_copy(which, src, dst, s, o):
        k = (q + o) % GROUP
        return pltpu.make_async_remote_copy(
            src_ref=src.at[k, s],
            dst_ref=dst.at[s, part_of(q)],
            send_sem=a2a_send.at[which, s, o],
            recv_sem=a2a_recv.at[which, s, o],
            device_id=group_peer(o),
            device_id_type=MESH,
        )

    cot_gather = functools.partial(gather_copy, 0, cot_hbm, cot_cols)
    back_spread = functools.partial(spread_copy, 1, back_send, back)
    act_gather = functools.partial(gather_copy, 2, active, act_cols)
    fwd_spread = functools.partial(spread_copy, 3, fwd_send, fwd)

    def start_all(copy, s):
        for o in range(1, GROUP):
            copy(s, o).start()

    def recv_all(copy, s):
        for o in range(1, GROUP):
            copy(s, o).wait_recv()

    for s in range(SLOTS):
        start_all(cot_gather, s)

    pools = ((x_top, x_bot, x_left, x_right), (g_top, g_bot, g_left, g_right))

    def halo_copies(f):
        def shift(axis, at, step):
            return {axis: (at + step + 4) % 4}

        def copy(k, src, dst, dev):
            return pltpu.make_async_remote_copy(
                src_ref=src,
                dst_ref=dst,
                send_sem=halo_send.at[f, k],
                recv_sem=halo_recv.at[f, k],
                device_id=dev,
                device_id_type=MESH,
            )

        result = []
        p_top, p_bot, p_left, p_right = pools[f]
        for k, (pool, axis, at, step) in enumerate(
            ((p_top, "gx", gx, 1), (p_bot, "gx", gx, -1), (p_left, "gy", gy, 1), (p_right, "gy", gy, -1))
        ):
            result.append(
                copy(k, pool.at[pl.ds(0, SLOTS)], pool.at[pl.ds(SLOTS, SLOTS)], shift(axis, at, step))
            )
        for k, (dx, dy) in enumerate(((1, 1), (1, -1), (-1, 1), (-1, -1))):
            dev = {**shift("gx", gx, dx), **shift("gy", gy, dy)}
            result.append(copy(4 + k, corner_send.at[f, k], corner_recv.at[f, k], dev))
        return result

    def own_pools(f):
        p_top, p_bot, p_left, p_right = pools[f]
        for s in range(SLOTS):
            p_bot[s] = pad[s, 1, 8 : 8 + LINE].astype(BF16)
            p_top[s] = pad[s, EDGE, 8 : 8 + LINE].astype(BF16)
            for x in range(EDGE):
                col0[ZS * x : ZS * x + ZS] = pad[s, 1 + x, 8:12]
                col1[ZS * x : ZS * x + ZS] = pad[s, 1 + x, 68:72]
            p_right[s] = col0[...].astype(BF16)
            p_left[s] = col1[...].astype(BF16)
            for k, (x, at) in enumerate(((EDGE, 68), (EDGE, 8), (1, 68), (1, 8))):
                corner_f[k, ZS * s : ZS * s + ZS] = pad[s, x, at : at + ZS]
        for k in range(4):
            corner_send[f, k] = corner_f[k].astype(BF16)
        for pool in (p_top, p_bot, p_left, p_right):
            pool[2 * SLOTS] = jnp.zeros((LINE, C), BF16)

    def entry(code, other):
        own = (code >= 16) & (code < 20)
        far = (code >= other) & (code < other + 4)
        return jnp.where(own, code - 16, jnp.where(far, code - other + 4, 8))

    def fill_halo(f, s):
        p_top, p_bot, p_left, p_right = pools[f]
        codes = [nbr_ref[s, d] for d in range(8)]
        pad[s, 0, 8 : 8 + LINE] = p_top[entry(codes[1], 4)].astype(F32)
        pad[s, EDGE + 1, 8 : 8 + LINE] = p_bot[entry(codes[6], 28)].astype(F32)
        col0[...] = p_left[entry(codes[3], 12)].astype(F32)
        col1[...] = p_right[entry(codes[4], 20)].astype(F32)
        for x in range(EDGE):
            pad[s, 1 + x, 4:8] = col0[ZS * x : ZS * x + ZS]
            pad[s, 1 + x, 72:76] = col1[ZS * x : ZS * x + ZS]
        for k, (d, row, at, pool_x, base_x, end_x, pool_y, base_y, end_y, base_c) in enumerate(
            (
                (0, 0, 4, p_top, 4, 1, p_left, 12, 1, 0),
                (2, 0, 72, p_top, 4, 0, p_right, 20, 1, 8),
                (5, EDGE + 1, 4, p_bot, 28, 1, p_left, 12, 0, 24),
                (7, EDGE + 1, 72, p_bot, 28, 0, p_right, 20, 0, 32),
            )
        ):
            code = codes[d]

            def piece(pool, base, end):
                low = (LINE - 16) * end
                rows = pool[entry(code, base), low : low + 16].astype(F32)
                return rows[12:16] if end else rows[0:4]

            via_x = piece(pool_x, base_x, end_x)
            via_y = piece(pool_y, base_y, end_y)
            tile = corner_recv[f, k].astype(F32)
            value = via_x
            value = jnp.where((code >= base_y) & (code < base_y + 4), via_y, value)
            for m in range(SLOTS):
                value = jnp.where(code == base_c + m, tile[ZS * m : ZS * m + ZS], value)
            pad[s, row, at : at + ZS] = value

    def lay_out(s, dst):
        for x in range(EDGE + 2):
            for j in range(3):
                at = 4 + ZS * j
                dst[s, x, :, C * j : C * j + C] = pad[s, x, at : at + LINE].astype(BF16)

    loads[0].wait()
    loads[5].wait()
    loads[6].wait()
    count = counts_ref[0, 0]

    def centre_x(s, carry):
        live = s < count
        for x in range(EDGE):
            rows = act_v[s, LINE * x : LINE * x + LINE].astype(F32)
            pad[s, 1 + x, 8 : 8 + LINE] = jnp.where(live, rows, 0.0)
        return carry

    lax.fori_loop(0, SLOTS, centre_x, 0)
    own_pools(0)
    x_halo = halo_copies(0)
    for copy in x_halo:
        copy.start()
    loads[2].wait()
    for i in range(3):
        for j in range(3):
            wbt[i, :, C * j : C * j + C] = w_v[3 * (2 - i) + 2 - j]

    for copy in x_halo:
        copy.wait_recv()

    def build_x(s, carry):
        fill_halo(0, s)
        lay_out(s, xcat)
        return carry

    lax.fori_loop(0, SLOTS, build_x, 0)

    def conv(n, carry):
        s = n // GROUP
        b = n % GROUP
        total = jnp.zeros((PART, C), F32)
        for i in range(3):
            window = xcat[s, pl.ds(4 * b + i, 4)].reshape(PART, 3 * C)
            weights = w_v[3 * i : 3 * i + 3].reshape(3 * C, C)
            total = total + jnp.dot(window, weights, preferred_element_type=F32)
        live = (s < count).astype(F32)
        sigma = jax.nn.sigmoid(total)
        active[s, part_of(b)] = (total * sigma * live).astype(BF16)
        dsilu[s, part_of(b)] = sigma * (1.0 + total * (1.0 - sigma)) * live
        return carry

    lax.fori_loop(0, SLOTS * GROUP, conv, 0)
    own_cols = pltpu.make_async_copy(active.at[:, part_of(q)], act_cols.at[q], load_sem.at[0])
    own_cols.start()

    loads[4].wait()
    taps = [dw_ref[t : t + 1].astype(F32) for t in range(5)]
    STEP = 32

    loads[3].wait()

    def depth_back(s):
        def step(n, carry):
            rows = pl.ds(pl.multiple_of(n * STEP, STEP), STEP)
            col = [cot_cols[k, s, rows].astype(F32) for k in range(GROUP)]
            for k in range(GROUP):
                total = None
                for t in range(5):
                    src = k - (t - 2)
                    if 0 <= src < GROUP:
                        term = taps[t] * col[src]
                        total = term if total is None else total + term
                back_send[k, s, rows] = total.astype(BF16)
            return carry

        lax.fori_loop(0, PART // STEP, step, 0)

    def do_back(s, carry):
        recv_all(cot_gather, s)
        depth_back(s)
        start_all(back_spread, s)
        back[s, part_of(q)] = back_send[q, s]
        return carry

    lax.fori_loop(0, SLOTS, do_back, 0)

    tacc[...] = jnp.zeros_like(tacc)

    def do_grad(s, carry):
        recv_all(back_spread, s)
        for x in range(EDGE):
            rows = pl.ds(LINE * x, LINE)
            grad = (back[s, rows].astype(F32) * dsilu[s, rows]).astype(BF16)
            gt[s, rows] = grad
            pad[s, 1 + x, 8 : 8 + LINE] = grad.astype(F32)
        return carry

    def tap_step(s, carry):
        grad_t = gt[s].T
        for i in range(3):
            window = xcat[s, i : i + EDGE].reshape(ROWS, 3 * C)
            tacc[i] += jnp.dot(grad_t, window, preferred_element_type=F32)
        return carry

    def grad_slot(s, carry):
        do_grad(s, 0)
        start_all(act_gather, s)
        tap_step(s, 0)
        return carry

    lax.fori_loop(0, SLOTS - 1, grad_slot, 0)
    do_grad(SLOTS - 1, 0)
    own_pools(1)
    g_halo = halo_copies(1)
    for copy in g_halo:
        copy.start()
    start_all(act_gather, SLOTS - 1)
    tap_step(SLOTS - 1, 0)
    for i in range(3):
        for j in range(3):
            block = tacc[i, :, C * j : C * j + C].T
            tp[:, 3 * i + j] = block.reshape(PLANE, 8, C)
    tp[:, TAPS] = jnp.zeros((PLANE, 8, C), F32)
    for p in range(PLANE):
        tp_send[p] = tp[p].reshape(PIECE, C).astype(BF16)

    def plane_scatter(j):
        p = (me_p + j) % PLANE
        return pltpu.make_async_remote_copy(
            src_ref=tp_send.at[p],
            dst_ref=rs_buf.at[me_p],
            send_sem=pl_send.at[0, j],
            recv_sem=pl_recv.at[0, j],
            device_id=p_peer(j),
            device_id_type=MESH,
        )

    def plane_gather(j):
        return pltpu.make_async_remote_copy(
            src_ref=tg_send,
            dst_ref=tg_hbm.at[me_p],
            send_sem=pl_send.at[1, j],
            recv_sem=pl_recv.at[1, j],
            device_id=p_peer(j),
            device_id_type=MESH,
        )

    def plane_depth(j):
        return pltpu.make_async_remote_copy(
            src_ref=dg_plane.at[me_p],
            dst_ref=dg_plane.at[me_p],
            send_sem=pl_send.at[2, j],
            recv_sem=pl_recv.at[2, j],
            device_id=p_peer(j),
            device_id_type=MESH,
        )

    def core_copy(n, src, dst):
        return pltpu.make_async_remote_copy(
            src_ref=src,
            dst_ref=dst,
            send_sem=core_send.at[n],
            recv_sem=core_recv.at[n],
            device_id=core_peer,
            device_id_type=MESH,
        )

    core_scatter = core_copy(0, z_src.at[pl.ds(HALF * (1 - core), HALF)], c_buf)
    core_gather = core_copy(1, z_all.at[pl.ds(HALF * core, HALF)], z_all.at[pl.ds(HALF * core, HALF)])
    core_depth = core_copy(2, dg_pair.at[core], dg_pair.at[core])

    def chip_copy(n, src, dst, j):
        return pltpu.make_async_remote_copy(
            src_ref=src,
            dst_ref=dst,
            send_sem=chip_send.at[n, j],
            recv_sem=chip_recv.at[n, j],
            device_id=chip_peer(j),
            device_id_type=MESH,
        )

    def chip_gather(j):
        return chip_copy(0, z_buf.at[chip], z_buf.at[chip], j)

    def chip_depth(j):
        return chip_copy(1, dg_z.at[chip], dg_z.at[chip], j)

    def each(copy, action, stop=PLANE):
        def step(j, carry):
            getattr(copy(j), action)()
            return carry

        lax.fori_loop(1, stop, step, 0)

    each(plane_scatter, "start")

    own_cols.wait()
    dg_acc[...] = jnp.zeros_like(dg_acc)

    def depth_forward(s):
        def step(n, carry):
            rows = pl.ds(pl.multiple_of(n * STEP, STEP), STEP)
            col = [act_cols[k, s, rows].astype(F32) for k in range(GROUP)]
            cot = [cot_cols[k, s, rows].astype(F32) for k in range(GROUP)]
            sums = [None] * 5
            for k in range(GROUP):
                total = None
                for t in range(5):
                    src = k + t - 2
                    if 0 <= src < GROUP:
                        term = taps[t] * col[src]
                        total = term if total is None else total + term
                        grad = col[src] * cot[k]
                        sums[t] = grad if sums[t] is None else sums[t] + grad
                fwd_send[k, s, rows] = total.astype(BF16)
            for t in range(5):
                dg_acc[t] += jnp.sum(sums[t].reshape(STEP // 8, 8, C), axis=0)
            return carry

        lax.fori_loop(0, PART // STEP, step, 0)

    def do_forward(s):
        recv_all(act_gather, s)
        depth_forward(s)
        start_all(fwd_spread, s)
        fwd[s, part_of(q)] = fwd_send[q, s]

    for copy in g_halo:
        copy.wait_recv()

    def build_g(s, carry):
        fill_halo(1, s)
        lay_out(s, gcat)
        return carry

    lax.fori_loop(0, SLOTS, build_g, 0)

    loads[1].wait()

    def conv_back(n, carry):
        s = n // GROUP
        b = n % GROUP
        total = jnp.zeros((PART, C), F32)
        for i in range(3):
            window = gcat[s, pl.ds(4 * b + i, 4)].reshape(PART, 3 * C)
            total = total + lax.dot_general(
                window, wbt[i], (((1,), (1,)), ((), ())), preferred_element_type=F32
            )
        live = (s < count).astype(F32)
        rows = part_of(b)
        cot_v[s, rows] = ((cot_v[s, rows].astype(F32) + total) * live).astype(BF16)
        return carry


    rs_buf[me_p] = tp_send[me_p]
    each(plane_scatter, "wait_recv")
    part_sum = rs_buf[0].astype(F32)
    for p in range(1, PLANE):
        part_sum = part_sum + rs_buf[p].astype(F32)
    z_src[...] = part_sum.reshape(2 * HALF, 8, C)
    core_scatter.start()
    core_scatter.wait_recv()
    z_own = (z_src[pl.ds(HALF * core, HALF)] + c_buf[...]).reshape(8 * HALF, C)
    z_buf[chip] = jnp.concatenate([z_own, jnp.zeros((ZPIECE - 8 * HALF, C), F32)], axis=0).astype(BF16)
    each(chip_gather, "start", CHIPS)
    do_forward(0)
    do_forward(1)
    lax.fori_loop(0, SLOTS * GROUP, conv_back, 0)
    ig_store = pltpu.make_async_copy(cot_v, ig_hbm, store_sem.at[0])
    ig_store.start()

    each(chip_gather, "wait_recv", CHIPS)
    z_sum = z_buf[0].astype(F32)
    for k in range(1, CHIPS):
        z_sum = z_sum + z_buf[k].astype(F32)
    z_all[pl.ds(HALF * core, HALF)] = z_sum[0 : 8 * HALF].reshape(HALF, 8, C)
    core_gather.start()
    core_gather.wait_recv()
    tg_send[...] = z_all[...].reshape(PIECE, C).astype(BF16)
    each(plane_gather, "start")
    tg_own = pltpu.make_async_copy(tg_send, tg_hbm.at[me_p], store_sem.at[1])
    tg_own.start()

    do_forward(2)
    do_forward(3)
    dg_pair[core] = jnp.concatenate(
        [jnp.sum(dg_acc[t], axis=0, keepdims=True) for t in range(5)] + [jnp.zeros((3, C), F32)], axis=0
    )
    core_depth.start()
    core_depth.wait_recv()
    dg_plane[me_p] = dg_pair[0] + dg_pair[1]
    each(plane_depth, "start")
    each(plane_depth, "wait_recv")
    dg_sum = dg_plane[0]
    for p in range(1, PLANE):
        dg_sum = dg_sum + dg_plane[p]
    dg_z[chip] = dg_sum
    each(chip_depth, "start", CHIPS)

    def out_store(s):
        return pltpu.make_async_copy(act_v.at[s], out_hbm.at[s], store_sem.at[2 + s])

    def finish(s, carry):
        recv_all(fwd_spread, s)
        live = s < count
        for b in range(GROUP):
            rows = pl.ds(PART * b, PART)
            masked = jnp.where(live, act_v[s, rows].astype(F32), 0.0)
            act_v[s, rows] = (masked + fwd[s, rows].astype(F32)).astype(BF16)
        out_store(s).start()
        return carry

    lax.fori_loop(0, SLOTS, finish, 0)
    each(chip_depth, "wait_recv", CHIPS)
    dg_all = dg_z[0]
    for k in range(1, CHIPS):
        dg_all = dg_all + dg_z[k]
    dg_out[...] = dg_all[0:5]
    dg_store = pltpu.make_async_copy(dg_out, dg_hbm, store_sem.at[6])
    dg_store.start()
    each(plane_gather, "wait_recv")

    for copy in x_halo + g_halo:
        copy.wait_send()
    for copy in (cot_gather, back_spread, act_gather, fwd_spread):
        for s in range(SLOTS):
            for o in range(1, GROUP):
                copy(s, o).wait_send()
    for copy in (plane_scatter, plane_gather, plane_depth):
        each(copy, "wait_send")
    for copy in (chip_gather, chip_depth):
        each(copy, "wait_send", CHIPS)
    for copy in (core_scatter, core_gather, core_depth):
        copy.wait_send()
    ig_store.wait()
    tg_own.wait()
    dg_store.wait()
    for s in range(SLOTS):
        out_store(s).wait()


def copy_out(*refs):
    src, dst, buf, tap_buf, load_sem, store_sem = refs[0:4], refs[4:8], refs[8:12], refs[12], refs[13], refs[14]
    loads = [pltpu.make_async_copy(src[2], buf[2], load_sem.at[0]), pltpu.make_async_copy(src[3], buf[3], load_sem.at[1])]
    stores = []
    for k in range(2):
        for s in range(SLOTS):
            n = 2 + SLOTS * k + s
            loads.append(pltpu.make_async_copy(src[k].at[s], buf[k].at[s], load_sem.at[n]))
            stores.append(pltpu.make_async_copy(buf[k].at[s], dst[k].at[s], store_sem.at[n]))
    stores += [pltpu.make_async_copy(tap_buf, dst[2], store_sem.at[0]), pltpu.make_async_copy(buf[3], dst[3], store_sem.at[1])]
    for load in loads:
        load.start()
    loads[0].wait()
    for p in range(PLANE):
        tap_buf[:, p] = buf[2][p].astype(F32)[0 : 8 * TAPS].reshape(TAPS, 8, C)
    stores[-2].start()
    loads[1].wait()
    stores[-1].start()
    for load, store in zip(loads[2:], stores[:-2]):
        load.wait()
        store.start()
    for store in stores:
        store.wait()


def body(activations, cotangent, tap_weights, depth_tap_weight, counts, neighbors):
    field = (SLOTS, ROWS, C)
    anywhere = pl.BlockSpec(memory_space=pl.ANY)
    results = pl.pallas_call(
        kernel,
        out_shape=[
            jax.ShapeDtypeStruct(field, BF16),
            jax.ShapeDtypeStruct(field, BF16),
            jax.ShapeDtypeStruct((PLANE, PIECE, C), BF16),
            jax.ShapeDtypeStruct((5, C), F32),
        ],
        in_specs=[anywhere] * 6,
        out_specs=[anywhere] * 4,
        scratch_shapes=[
            pltpu.SMEM((1, 1), jnp.int32),
            pltpu.SMEM((SLOTS, 8), jnp.int32),
            pltpu.VMEM(field, BF16),
            pltpu.VMEM(field, BF16),
            pltpu.VMEM((TAPS, C, C), BF16),
            pltpu.VMEM((5, C), BF16),
            pltpu.VMEM((3, C, 3 * C), BF16),
            pltpu.VMEM((SLOTS, EDGE + 2, LINE + 16, C), F32),
            pltpu.VMEM((SLOTS, EDGE + 2, LINE, 3 * C), BF16),
            pltpu.VMEM((SLOTS, EDGE + 2, LINE, 3 * C), BF16),
            pltpu.VMEM(field, BF16),
            pltpu.VMEM(field, F32),
            pltpu.VMEM(field, BF16),
            pltpu.VMEM((GROUP, SLOTS, PART, C), BF16),
            pltpu.VMEM((GROUP, SLOTS, PART, C), BF16),
            pltpu.VMEM(field, BF16),
            pltpu.VMEM((GROUP, SLOTS, PART, C), BF16),
            pltpu.VMEM((GROUP, SLOTS, PART, C), BF16),
            pltpu.VMEM(field, BF16),
            pltpu.VMEM((2 * SLOTS + 1, LINE, C), BF16),
            pltpu.VMEM((2 * SLOTS + 1, LINE, C), BF16),
            pltpu.VMEM((2 * SLOTS + 1, LINE, C), BF16),
            pltpu.VMEM((2 * SLOTS + 1, LINE, C), BF16),
            pltpu.VMEM((2 * SLOTS + 1, LINE, C), BF16),
            pltpu.VMEM((2 * SLOTS + 1, LINE, C), BF16),
            pltpu.VMEM((2 * SLOTS + 1, LINE, C), BF16),
            pltpu.VMEM((2 * SLOTS + 1, LINE, C), BF16),
            pltpu.VMEM((2, 4, 16, C), BF16),
            pltpu.VMEM((2, 4, 16, C), BF16),
            pltpu.VMEM((LINE, C), F32),
            pltpu.VMEM((LINE, C), F32),
            pltpu.VMEM((4, 16, C), F32),
            pltpu.VMEM((3, C, 3 * C), F32),
            pltpu.VMEM((PLANE, 2 * HALF, 8, C), F32),
            pltpu.VMEM((PLANE, PIECE, C), BF16),
            pltpu.VMEM((PLANE, PIECE, C), BF16),
            pltpu.VMEM((2 * HALF, 8, C), F32),
            pltpu.VMEM((HALF, 8, C), F32),
            pltpu.VMEM((CHIPS, ZPIECE, C), BF16),
            pltpu.VMEM((2 * HALF, 8, C), F32),
            pltpu.VMEM((PIECE, C), BF16),
            pltpu.VMEM((5, 8, C), F32),
            pltpu.VMEM((2, 8, C), F32),
            pltpu.VMEM((PLANE, 8, C), F32),
            pltpu.VMEM((CHIPS, 8, C), F32),
            pltpu.VMEM((5, C), F32),
            pltpu.SemaphoreType.DMA((7,)),
            pltpu.SemaphoreType.DMA((7,)),
            pltpu.SemaphoreType.DMA((2, 8)),
            pltpu.SemaphoreType.DMA((2, 8)),
            pltpu.SemaphoreType.DMA((4, SLOTS, GROUP)),
            pltpu.SemaphoreType.DMA((4, SLOTS, GROUP)),
            pltpu.SemaphoreType.DMA((3, PLANE)),
            pltpu.SemaphoreType.DMA((3, PLANE)),
            pltpu.SemaphoreType.DMA((3,)),
            pltpu.SemaphoreType.DMA((3,)),
            pltpu.SemaphoreType.DMA((2, CHIPS)),
            pltpu.SemaphoreType.DMA((2, CHIPS)),
        ],
        compiler_params=pltpu.CompilerParams(
            collective_id=0, has_side_effects=True, vmem_limit_bytes=60 * 2**20
        ),
        name="unet_section",
    )(
        counts,
        neighbors.reshape(SLOTS, 8),
        activations.reshape(field),
        cotangent.reshape(field),
        tap_weights,
        depth_tap_weight,
    )
    output, input_grad, tap_grad, depth_grad = pl.pallas_call(
        copy_out,
        out_shape=[
            jax.ShapeDtypeStruct(field, BF16),
            jax.ShapeDtypeStruct(field, BF16),
            jax.ShapeDtypeStruct((TAPS, PLANE, 8, C), F32),
            jax.ShapeDtypeStruct((5, C), F32),
        ],
        in_specs=[anywhere] * 4,
        out_specs=[anywhere] * 4,
        scratch_shapes=[pltpu.VMEM(r.shape, r.dtype) for r in results]
        + [
            pltpu.VMEM((TAPS, PLANE, 8, C), F32),
            pltpu.SemaphoreType.DMA((10,)),
            pltpu.SemaphoreType.DMA((10,)),
        ],
        compiler_params=pltpu.CompilerParams(vmem_limit_bytes=60 * 2**20),
        name="copy_out",
    )(*results)
    return (
        output.reshape(activations.shape),
        input_grad.reshape(activations.shape),
        tap_grad.reshape(TAPS, C, C),
        depth_grad,
    )


def solution(mesh):
    field = P("gx", "gy", None, None, None, "gz", None)
    return jax.shard_map(
        body,
        mesh=mesh,
        in_specs=(field, field, P(), P(), P("gx", "gy"), P("gx", "gy", None, None)),
        out_specs=(field, field, P(), P()),
        check_vma=False,
    )
```
